32 devices in a mesh: layer: 8 (over z, x), width: 4 (over y, core).
Axes of the slice: x: 2, y: 2, z: 4, core: 2. Of those that a mesh axis runs over, the one named last changes fastest.
Arguments:
- mlp_inputs: bfloat16 [8, 768, 4096], P('layer', None, 'width'), may hold values from -6 to 6
- mlp_outputs: bfloat16 [8, 768, 4096], P('layer', None, 'width'), may hold values from -6 to 6
- encoders: bfloat16 [8, 4096, 128], P('layer', 'width'), may hold values from -0.09375 to 0.09375
- encoder_bias: float32 [8, 128], P('layer'), may hold values from -0.5 to 0
- decoders: bfloat16 [8, 8, 128, 4096], P('layer', None, None, 'width'), may hold values from -0.1875 to 0.1875
Outputs:
- loss_mean: float32 [], replicated
- grad_encoders: bfloat16 [8, 4096, 128], P('layer', 'width')
- grad_encoder_bias: float32 [8, 128], P('layer')
- grad_decoders: bfloat16 [8, 8, 128, 4096], P('layer', None, None, 'width')
The draws below stay inside these ranges and needn't reach their ends.
All inputs are finite; a program needn't handle non-finite values.
Results may differ from the reference program's by a relative error of at most 0.0055.
Values may be sent and summed in bfloat16 or wider, within the bound.
A program may use at most 128 MiB of HBM per device.

```python
import jax
import jax.numpy as jnp
from jax import lax

D = 4096
LATENT_WIDTH = 128
TOKENS = 768
DEPTH_TOTAL = 8


def steps_of(key, dims, cuts, least, top_value):
    def one(axis_at, parts):
        draws = jax.random.uniform(jax.random.fold_in(jax.random.fold_in(key, 6), axis_at), (parts,), jnp.float32, least / len(cuts), top_value / len(cuts))
        return jnp.repeat(jnp.exp(draws), dims[axis_at] // parts).reshape((-1,) + (1,) * (len(dims) - axis_at - 1))

    loudness = one(*cuts[0])
    for cut in cuts[1:]:
        loudness = loudness * one(*cut)
    return loudness


def gaussian(rng, dims, deviation, limit, shards=(), kind=jnp.bfloat16):
    values = deviation * jax.random.normal(rng, dims, jnp.float32)
    if shards:
        values = values * steps_of(rng, dims, shards, -0.22, 0.18)
    return jnp.clip(values, -limit, limit).astype(kind)


def setup_inputs(seed: int = 0) -> dict:
    splits = jax.random.split(jax.random.key(seed), 6)
    mlp_inputs = gaussian(splits[0], (DEPTH_TOTAL, TOKENS, D), 1.0, 6.0, ((0, 8), (2, 4)))
    mlp_outputs = gaussian(splits[1], (DEPTH_TOTAL, TOKENS, D), 1.0, 6.0, ((0, 8), (2, 4)))
    encoders = gaussian(splits[2], (DEPTH_TOTAL, D, LATENT_WIDTH), D ** -0.5, 0.09375, ((0, 8), (1, 4)))
    encoder_bias = jnp.clip(-0.5 + 0.5 * jax.random.uniform(splits[3], (DEPTH_TOTAL, LATENT_WIDTH), jnp.float32) ** steps_of(splits[3], (DEPTH_TOTAL, LATENT_WIDTH), ((0, 8),), -0.2, 0.2), -0.5, 0.0)
    decoders = gaussian(splits[4], (DEPTH_TOTAL, DEPTH_TOTAL, LATENT_WIDTH, D), (LATENT_WIDTH * 8) ** -0.5, 0.1875, ((0, 8), (3, 4)))
    return dict(mlp_inputs=mlp_inputs, mlp_outputs=mlp_outputs, encoders=encoders, encoder_bias=encoder_bias, decoders=decoders)


sparsity = 8.0

def reference(mlp_inputs, mlp_outputs, encoders, encoder_bias, decoders):
    position_vectors = mlp_inputs.shape[1]

    def encode(pair):
        return jnp.dot(pair[0], pair[1], preferred_element_type=jnp.float32)
    potential = lax.map(encode, (mlp_inputs, encoders)) + encoder_bias[:, None, :]
    nonzero_latents = jnp.maximum(potential, 0.0)
    positive_indicator = nonzero_latents.astype(jnp.bfloat16)
    merged_positions = jnp.transpose(positive_indicator, (1, 0, 2)).reshape(position_vectors, DEPTH_TOTAL * LATENT_WIDTH)
    sources = jnp.arange(DEPTH_TOTAL, dtype=jnp.int32)

    def target_step(running, inputs):
        target, decoder, wanted = inputs
        columns = jnp.repeat(sources <= target, LATENT_WIDTH)
        masked = merged_positions * columns.astype(jnp.bfloat16)[None, :]
        weights = decoder.reshape(DEPTH_TOTAL * LATENT_WIDTH, D)
        rebuilt = jnp.dot(masked, weights, preferred_element_type=jnp.float32)
        misfit = rebuilt - wanted.astype(jnp.float32)
        signal = (misfit / position_vectors).astype(jnp.bfloat16)
        backward = jnp.dot(signal, weights.T, preferred_element_type=jnp.float32)
        backward = backward * columns.astype(jnp.float32)[None, :]
        grad_block = jnp.dot(masked.T, signal, preferred_element_type=jnp.float32)
        grad_block = grad_block.astype(jnp.bfloat16).reshape(DEPTH_TOTAL, LATENT_WIDTH, D)
        return (running + backward, (0.5 * jnp.sum(misfit * misfit), grad_block))
    start_total = jnp.zeros((position_vectors, DEPTH_TOTAL * LATENT_WIDTH), jnp.float32)
    targets = jnp.arange(DEPTH_TOTAL, dtype=jnp.int32)
    summed, outputs = lax.scan(target_step, start_total, (targets, decoders, mlp_outputs))
    squares, grad_decoders = outputs
    feature_grad = jnp.transpose(summed.reshape(position_vectors, DEPTH_TOTAL, LATENT_WIDTH), (1, 0, 2))
    delta = (feature_grad + sparsity / position_vectors) * (potential > 0).astype(jnp.float32)

    def encoder_grad(pair):
        return lax.dot_general(pair[0], pair[1].astype(jnp.bfloat16), (((0,), (0,)), ((), ())), preferred_element_type=jnp.float32).astype(jnp.bfloat16)
    grad_encoders = lax.map(encoder_grad, (mlp_inputs, delta))
    grad_encoder_bias = lax.optimization_barrier(jnp.sum(delta, axis=1))
    loss_mean = (jnp.sum(squares) + sparsity * jnp.sum(nonzero_latents)) / (position_vectors * D * DEPTH_TOTAL)
    return (loss_mean, grad_encoders, grad_encoder_bias, grad_decoders)
```

```python
import functools

import jax
import jax.numpy as jnp
from jax import lax
from jax.experimental import pallas as pl
from jax.experimental.pallas import tpu as pltpu
from jax.sharding import PartitionSpec as P

SPARSITY = 8.0
MESH = pl.DeviceIdType.MESH
F32 = jnp.float32
BF16 = jnp.bfloat16


def dot_nn(a, b):
    return jnp.dot(a, b, preferred_element_type=F32)


def dot_nt(a, b):
    return lax.dot_general(a, b, (((1,), (1,)), ((), ())), preferred_element_type=F32)


def kernel(
    layers, widths,
    x_hbm, t_hbm, e_hbm, b_ref, d_hbm,
    loss_ref, ge_ref, gb_ref, gd_hbm,
    x, xt, t, enc, dec, acc, sig, fire, fire_t, pot,
    ea_send, ea_recv, ey_send, ey_recv,
    c_send, c_recv, c_own, cy_send, cy_recv, cd_send, cd_recv, fg,
    delta, gb_all, loss_w, loss_l, gd, zero,
    in_sems, x_sems, out_sems, ea_s, ea_r, ey_s, ey_r,
    fd_s, fd_r, fy_s, fy_r, fs_s, fs_r, ff_s, ff_r,
    cs_s, cs_r, cy_s, cy_r, cd_s, cd_r,
    dl_s, dl_r, gb_s, gb_r, lw_s, lw_r, ll_s, ll_r,
):
    tokens, depth = x.shape
    lat = enc.shape[1]
    half, quarter = tokens // 2, tokens // 4
    me = lax.axis_index("layer")
    w = lax.axis_index("width")
    core, y = lax.rem(w, 2), lax.div(w, 2)
    sib = (me, w + 1 - 2 * core)
    ynb = (me, w + 2 - 4 * y)

    def rows(c_at, y_at):
        return pl.ds(pl.multiple_of(c_at * half + y_at * quarter, 16), quarter)

    def remote(src, dst, send_sem, recv_sem, where):
        return pltpu.make_async_remote_copy(
            src_ref=src, dst_ref=dst, send_sem=send_sem, recv_sem=recv_sem,
            device_id=where, device_id_type=MESH,
        )

    own_rows = rows(core, y)
    ynb_rows = rows(core, 1 - y)
    sib_rows = rows(1 - core, y)
    diag_rows = rows(1 - core, 1 - y)

    order = (diag_rows, sib_rows, ynb_rows, own_rows)
    cp_enc = pltpu.make_async_copy(e_hbm.at[0], enc, in_sems.at[0])
    cp_enc.start()
    cp_x = [pltpu.make_async_copy(x_hbm.at[0, r], x.at[r], x_sems.at[k]) for k, r in enumerate(order)]
    for cp in cp_x:
        cp.start()
    cp_t = pltpu.make_async_copy(t_hbm.at[0], t, in_sems.at[1])
    cp_t.start()
    cp_dec = pltpu.make_async_copy(d_hbm.at[0], dec, in_sems.at[2])
    cp_dec.start()

    barrier = pltpu.get_barrier_semaphore()

    def greet_layer(k, carry):
        pl.semaphore_signal(barrier, inc=1, device_id=(lax.rem(me + k, layers), w), device_id_type=MESH)
        return carry

    def greet_width(k, carry):
        pl.semaphore_signal(barrier, inc=1, device_id=(me, lax.rem(w + k, widths)), device_id_type=MESH)
        return carry

    lax.fori_loop(1, layers, greet_layer, 0)
    lax.fori_loop(1, widths, greet_width, 0)

    cp_enc.wait()
    cp_ea = [remote(ea_send.at[k], ea_recv.at[k], ea_s.at[k], ea_r.at[k], sib) for k in range(2)]
    for k in range(2):
        cp_x[k].wait()
        ea_send[k] = dot_nn(x[order[k], :], enc[...])
        if k == 0:
            pl.semaphore_wait(barrier, layers - 1 + widths - 1)
        cp_ea[k].start()
    cp_x[2].wait()
    part = dot_nn(x[ynb_rows, :], enc[...])
    cp_ea[0].wait_recv()
    ey_send[...] = part + ea_recv[0]
    cp_ey = remote(ey_send, ey_recv, ey_s.at[0], ey_r.at[0], ynb)
    cp_ey.start()
    cp_x[3].wait()
    part = dot_nn(x[own_rows, :], enc[...])
    cp_ea[1].wait_recv()
    part = part + ea_recv[1]
    cp_ey.wait_recv()
    potential = part + ey_recv[...] + b_ref[...]
    pot[...] = potential
    active = jnp.maximum(potential, 0.0)
    fire[me, own_rows, :] = active.astype(BF16)
    active_sum = jnp.sum(active.reshape(quarter // 8, 8, lat), axis=0)

    pair = lax.div(me, 2)

    @pl.when(lax.rem(me, 2) == 0)
    def _():
        fire[me + 1, own_rows, :] = jnp.zeros((quarter, lat), BF16)

    def fire_copy(src_layer, dst_layer):
        ref = fire.at[src_layer, own_rows, :]
        return remote(ref, ref, fd_s.at[dst_layer], fd_r.at[src_layer], (dst_layer, w))

    def send_fire(m, carry):
        fire_copy(me, m).start()
        return carry

    lax.fori_loop(me + 1, layers, send_fire, 0)

    def fire_pair(p, r, send, recv, where):
        ref = fire.at[pl.ds(2 * p, 2), r, :]
        return remote(ref, ref, send.at[p], recv.at[p], where)

    zero[...] = jnp.zeros(zero.shape, BF16)

    def zero_copy(p):
        return pltpu.make_async_copy(zero, gd_hbm.at[0, pl.ds(2 * p, 2)], out_sems.at[p])

    def send_zero(p, carry):
        zero_copy(p).start()
        return carry

    lax.fori_loop(pair + 1, layers // 2, send_zero, 0)

    def stage_far(p):
        for j in range(2):
            @pl.when(2 * p + j < me)
            def _():
                fire_copy(2 * p + j, me).wait_recv()
        fire_pair(p, own_rows, fy_s, fy_r, ynb).start()
        fire_pair(p, own_rows, fs_s, fs_r, sib).start()

    def stage_y(p):
        fire_pair(p, ynb_rows, fy_s, fy_r, ynb).wait_recv()
        fire_pair(p, ynb_rows, ff_s, ff_r, sib).start()

    cp_t.wait()
    blk = 128 if tokens % 128 == 0 else 16

    def prepare(k, carry):
        r = pl.ds(pl.multiple_of(k * blk, blk), blk)
        acc[r, :] = -t[r, :].astype(F32)
        return carry

    lax.fori_loop(0, tokens // blk, prepare, 0)

    @pl.when(lax.rem(me, 2) == 0)
    def _():
        stage_far(pair)

    for k in range(0, depth, 256):
        xt[k:k + 256, :] = x[:, k:k + 256].T
    cp_dec.wait()

    cols = 512 if depth % 512 == 0 else 128

    def features(p):
        return jnp.concatenate([fire[2 * p], fire[2 * p + 1]], axis=-1)

    def weights(p, at):
        return dec[pl.ds(2 * p, 2), :, at].reshape(2 * lat, -1)

    def forward(i, carry):
        @pl.when((i <= pair) & ((i > 0) | (lax.rem(me, 2) == 1)))
        def _():
            stage_far(pair - i)

        @pl.when((i >= 1) & (i <= pair + 1))
        def _():
            stage_y(pair - i + 1)

        @pl.when(i >= 2)
        def _():
            p = pair - i + 2
            fire_pair(p, sib_rows, fs_s, fs_r, sib).wait_recv()
            fire_pair(p, diag_rows, ff_s, ff_r, sib).wait_recv()
            f = features(p)
            for n in range(0, depth, cols):
                at = slice(n, n + cols)
                acc[:, at] += dot_nn(f, weights(p, at))
            fire_t[p] = f.T
        return carry

    lax.fori_loop(0, pair + 3, forward, 0)

    def finish(k, total):
        r = pl.ds(pl.multiple_of(k * blk, blk), blk)
        m = acc[r, :]
        sig[r, :] = (m * (1.0 / tokens)).astype(BF16)
        sq = jnp.sum((m * m).reshape(blk // 8, 8, depth), axis=0)
        return total + sum(sq[:, n:n + lat] for n in range(0, depth, lat))

    squares = lax.fori_loop(0, tokens // blk, finish, jnp.zeros((8, lat), F32))
    loss_w[w] = 0.5 * squares + SPARSITY * active_sum

    def width_copy(ref, send, recv, src, dst):
        return remote(ref.at[src], ref.at[src], send.at[dst], recv.at[src], (me, dst))

    for k in range(1, widths):
        width_copy(loss_w, lw_s, lw_r, w, lax.rem(w + k, widths)).start()

    own_half = pl.ds(pl.multiple_of(core * half, 16), half)
    sib_half = pl.ds(pl.multiple_of((1 - core) * half, 16), half)
    keep = pl.ds(pl.multiple_of(y * quarter, 16), quarter)
    give = pl.ds(pl.multiple_of((1 - y) * quarter, 16), quarter)

    def c_copy(p):
        return remote(c_send.at[p], c_recv.at[p], cs_s.at[p], cs_r.at[p], sib)

    def cy_copy(p):
        return remote(cy_send.at[p], cy_recv.at[p], cy_s.at[p], cy_r.at[p], ynb)

    def cd_copy(src_layer, dst_layer):
        return remote(
            cd_send.at[dst_layer], cd_recv.at[src_layer], cd_s.at[dst_layer], cd_r.at[src_layer], (dst_layer, w)
        )

    def gd_copy(p):
        return pltpu.make_async_copy(gd.at[pl.ds(2 * p, 2)], gd_hbm.at[0, pl.ds(2 * p, 2)], out_sems.at[p])

    every = slice(0, depth)

    def backward(i, carry):
        @pl.when(i <= pair)
        def _():
            p = i
            out = dot_nt(sig[sib_half, :], weights(p, every)).astype(BF16)
            for j in range(2):
                c_send[p, j] = out[:, j * lat:(j + 1) * lat]
            c_copy(p).start()
            out = dot_nt(sig[own_half, :], weights(p, every))
            for j in range(2):
                c_own[p, j] = out[:, j * lat:(j + 1) * lat]

        @pl.when((i >= 1) & (i <= pair + 1))
        def _():
            p = i - 1
            c_copy(p).wait_recv()
            for j in range(2):
                cy_send[p, j] = (c_own[p, j, give, :] + c_recv[p, j, give, :].astype(F32)).astype(BF16)
            cy_copy(p).start()

        @pl.when(i <= pair)
        def _():
            p = i
            for n in range(0, depth, cols):
                at = slice(n, n + cols)
                gd[pl.ds(2 * p, 2), :, at] = dot_nn(fire_t[p], sig[:, at]).astype(BF16).reshape(2, lat, cols)
            gd_copy(p).start()

        @pl.when(i >= 2)
        def _():
            p = i - 2
            cy_copy(p).wait_recv()
            for j in range(2):
                l = 2 * p + j
                total = c_own[p, j, keep, :] + c_recv[p, j, keep, :].astype(F32) + cy_recv[p, j].astype(F32)

                @pl.when(l < me)
                def _():
                    cd_send[l] = total.astype(BF16)
                    cd_copy(me, l).start()

                @pl.when(l == me)
                def _():
                    fg[...] = total
        return carry

    lax.fori_loop(0, pair + 3, backward, 0)

    for k in range(1, widths):
        width_copy(loss_w, lw_s, lw_r, lax.rem(w + k, widths), w).wait_recv()
    total = loss_w[0]
    for k in range(1, widths):
        total = total + loss_w[k]
    loss_l[me] = total

    def layer_copy(src, dst):
        return remote(loss_l.at[src], loss_l.at[src], ll_s.at[dst], ll_r.at[src], (dst, w))

    def send_loss(k, carry):
        layer_copy(me, lax.rem(me + k, layers)).start()
        return carry

    lax.fori_loop(1, layers, send_loss, 0)

    def gather(m, carry):
        cd_copy(m, me).wait_recv()
        fg[...] += cd_recv[m].astype(F32)
        return carry

    lax.fori_loop(me + 1, layers, gather, 0)

    d = jnp.where(pot[...] > 0, fg[...] + SPARSITY / tokens, 0.0)
    delta[own_rows, :] = d.astype(BF16)

    def delta_copy(r, k, where):
        return remote(delta.at[r, :], delta.at[r, :], dl_s.at[k], dl_r.at[k], where)

    delta_copy(own_rows, 0, ynb).start()
    delta_copy(own_rows, 1, sib).start()
    gb_all[w] = jnp.sum(d.reshape(quarter // 8, 8, lat), axis=0)
    for k in range(1, widths):
        width_copy(gb_all, gb_s, gb_r, w, lax.rem(w + k, widths)).start()
    delta_copy(ynb_rows, 0, ynb).wait_recv()
    delta_copy(ynb_rows, 2, sib).start()

    def take_loss(k, carry):
        layer_copy(lax.rem(me + k, layers), me).wait_recv()
        return carry

    lax.fori_loop(1, layers, take_loss, 0)
    loss = lax.fori_loop(0, layers, lambda k, s: s + loss_l[k], jnp.zeros((8, lat), F32))
    loss_ref[0, 0] = jnp.sum(loss) / (tokens * depth * widths * layers)

    delta_copy(sib_rows, 1, sib).wait_recv()
    delta_copy(diag_rows, 2, sib).wait_recv()
    ge_ref[0] = dot_nn(xt[...], delta[...]).astype(BF16)
    for k in range(1, widths):
        width_copy(gb_all, gb_s, gb_r, lax.rem(w + k, widths), w).wait_recv()
    bias = gb_all[0]
    for k in range(1, widths):
        bias = bias + gb_all[k]
    gb_ref[...] = jnp.sum(bias, axis=0, keepdims=True)

    for cp in cp_ea:
        cp.wait_send()
    cp_ey.wait_send()

    def drain_fire(m, carry):
        fire_copy(me, m).wait_send()
        return carry

    lax.fori_loop(me + 1, layers, drain_fire, 0)

    def drain_pair(p, carry):
        fire_pair(p, own_rows, fy_s, fy_r, ynb).wait_send()
        fire_pair(p, own_rows, fs_s, fs_r, sib).wait_send()
        fire_pair(p, ynb_rows, ff_s, ff_r, sib).wait_send()
        c_copy(p).wait_send()
        cy_copy(p).wait_send()
        gd_copy(p).wait()
        return carry

    lax.fori_loop(0, pair + 1, drain_pair, 0)

    def drain_zero(p, carry):
        zero_copy(p).wait()
        return carry

    lax.fori_loop(pair + 1, layers // 2, drain_zero, 0)

    def drain_grad(l, carry):
        cd_copy(me, l).wait_send()
        return carry

    lax.fori_loop(0, me, drain_grad, 0)

    def drain_loss(k, carry):
        layer_copy(me, lax.rem(me + k, layers)).wait_send()
        return carry

    lax.fori_loop(1, layers, drain_loss, 0)
    for k in range(1, widths):
        other = lax.rem(w + k, widths)
        width_copy(loss_w, lw_s, lw_r, w, other).wait_send()
        width_copy(gb_all, gb_s, gb_r, w, other).wait_send()
    delta_copy(own_rows, 0, ynb).wait_send()
    delta_copy(own_rows, 1, sib).wait_send()
    delta_copy(ynb_rows, 2, sib).wait_send()


def per_device(x, t, e, b, d):
    layers, widths = lax.axis_size("layer"), lax.axis_size("width")
    tokens, depth = x.shape[1:]
    lat = e.shape[2]
    half, quarter = tokens // 2, tokens // 4
    pairs = layers // 2
    vmem = pltpu.VMEM
    sem = pltpu.SemaphoreType.DMA
    scratch = [
        vmem((tokens, depth), BF16),
        vmem((depth, tokens), BF16),
        vmem((tokens, depth), BF16),
        vmem((depth, lat), BF16),
        vmem((layers, lat, depth), BF16),
        vmem((tokens, depth), F32),
        vmem((tokens, depth), BF16),
        vmem((layers, tokens, lat), BF16),
        vmem((pairs, 2 * lat, tokens), BF16),
        vmem((quarter, lat), F32),
        vmem((2, quarter, lat), F32),
        vmem((2, quarter, lat), F32),
        vmem((quarter, lat), F32),
        vmem((quarter, lat), F32),
        vmem((pairs, 2, half, lat), BF16),
        vmem((pairs, 2, half, lat), BF16),
        vmem((pairs, 2, half, lat), F32),
        vmem((pairs, 2, quarter, lat), BF16),
        vmem((pairs, 2, quarter, lat), BF16),
        vmem((layers, quarter, lat), BF16),
        vmem((layers, quarter, lat), BF16),
        vmem((quarter, lat), F32),
        vmem((tokens, lat), BF16),
        vmem((widths, 8, lat), F32),
        vmem((widths, 8, lat), F32),
        vmem((layers, 8, lat), F32),
        vmem((layers, lat, depth), BF16),
        vmem((2, lat, depth), BF16),
    ]
    scratch += [
        sem((3,)), sem((4,)), sem((pairs,)), sem((2,)), sem((2,)), sem((1,)), sem((1,)),
        sem((layers,)), sem((layers,)), sem((pairs,)), sem((pairs,)),
        sem((pairs,)), sem((pairs,)), sem((pairs,)), sem((pairs,)),
        sem((pairs,)), sem((pairs,)), sem((pairs,)), sem((pairs,)), sem((layers,)), sem((layers,)),
        sem((3,)), sem((3,)), sem((widths,)), sem((widths,)), sem((widths,)), sem((widths,)),
        sem((layers,)), sem((layers,)),
    ]
    anyspace = pl.BlockSpec(memory_space=pl.ANY)
    vspace = pl.BlockSpec(memory_space=pltpu.VMEM)
    loss, ge, gb, gd = pl.pallas_call(
        functools.partial(kernel, layers, widths),
        out_shape=(
            jax.ShapeDtypeStruct((1, 1), F32),
            jax.ShapeDtypeStruct((1, depth, lat), BF16),
            jax.ShapeDtypeStruct((1, lat), F32),
            jax.ShapeDtypeStruct((1, layers, lat, depth), BF16),
        ),
        in_specs=[anyspace, anyspace, anyspace, vspace, anyspace],
        out_specs=(pl.BlockSpec(memory_space=pltpu.SMEM), vspace, vspace, anyspace),
        scratch_shapes=scratch,
        compiler_params=pltpu.CompilerParams(
            collective_id=0, has_side_effects=True, vmem_limit_bytes=60 * 1024 * 1024
        ),
        cost_estimate=pl.CostEstimate(
            flops=6 * tokens * depth * layers * lat, bytes_accessed=4 * layers * lat * depth, transcendentals=0
        ),
    )(x, t, e, b, d)
    return loss.reshape(()), ge, gb, gd


def solution(mesh):
    return jax.shard_map(
        per_device,
        mesh=mesh,
        in_specs=(
            P("layer", None, "width"),
            P("layer", None, "width"),
            P("layer", "width", None),
            P("layer", None),
            P("layer", None, None, "width"),
        ),
        out_specs=(
            P(),
            P("layer", "width", None),
            P("layer", None),
            P("layer", None, None, "width"),
        ),
        check_vma=False,
    )
```

```python
import functools
import math

import jax
import jax.numpy as jnp
from jax import lax
from jax.experimental import pallas as pl
from jax.experimental.pallas import tpu as pltpu
from jax.sharding import PartitionSpec as P

SPARSITY = 8.0
MESH = pl.DeviceIdType.MESH
F32 = jnp.float32
BF16 = jnp.bfloat16


def dot_nn(a, b):
    return jnp.dot(a, b, preferred_element_type=F32)


def dot_nt(a, b):
    return lax.dot_general(a, b, (((1,), (1,)), ((), ())), preferred_element_type=F32)


def kernel(
    layers, widths,
    x_hbm, t_hbm, e_hbm, b_ref, d_hbm,
    loss_ref, ge_ref, gb_ref, gd_hbm,
    x, xt, t, enc, dec, acc, sig, fire, fire_t, pot,
    ea_send, ea_recv, ey_send, ey_recv,
    c_send, c_recv, c_own, cy_send, cy_recv, cd_send, cd_recv, fg,
    delta, gb_all, loss_w, loss_l, gd, zero,
    in_sems, x_sems, out_sems, ea_s, ea_r, ey_s, ey_r,
    fd_s, fd_r, fy_s, fy_r, fs_s, fs_r, ff_s, ff_r,
    cs_s, cs_r, cy_s, cy_r, cd_s, cd_r,
    dl_s, dl_r, gb_s, gb_r, lw_s, lw_r, ll_s, ll_r,
):
    tokens, depth = x.shape
    lat = enc.shape[1]
    half, quarter = tokens // 2, tokens // 4
    me = lax.axis_index("layer")
    w = lax.axis_index("width")
    core, y = lax.rem(w, 2), lax.div(w, 2)
    sib = (me, w + 1 - 2 * core)
    ynb = (me, w + 2 - 4 * y)

    def rows(c_at, y_at):
        return pl.ds(pl.multiple_of(c_at * half + y_at * quarter, 16), quarter)

    def remote(src, dst, send_sem, recv_sem, where):
        return pltpu.make_async_remote_copy(
            src_ref=src, dst_ref=dst, send_sem=send_sem, recv_sem=recv_sem,
            device_id=where, device_id_type=MESH,
        )

    own_rows = rows(core, y)
    ynb_rows = rows(core, 1 - y)
    sib_rows = rows(1 - core, y)
    diag_rows = rows(1 - core, 1 - y)

    order = (diag_rows, sib_rows, ynb_rows, own_rows)
    cp_enc = pltpu.make_async_copy(e_hbm.at[0], enc, in_sems.at[0])
    cp_enc.start()
    cp_x = [pltpu.make_async_copy(x_hbm.at[0, r], x.at[r], x_sems.at[k]) for k, r in enumerate(order)]
    for cp in cp_x:
        cp.start()
    cp_t = pltpu.make_async_copy(t_hbm.at[0], t, in_sems.at[1])
    cp_t.start()
    cp_dec = pltpu.make_async_copy(d_hbm.at[0], dec, in_sems.at[2])
    cp_dec.start()

    barrier = pltpu.get_barrier_semaphore()

    def greet_layer(k, carry):
        pl.semaphore_signal(barrier, inc=1, device_id=(lax.rem(me + k, layers), w), device_id_type=MESH)
        return carry

    def greet_width(k, carry):
        pl.semaphore_signal(barrier, inc=1, device_id=(me, lax.rem(w + k, widths)), device_id_type=MESH)
        return carry

    lax.fori_loop(1, layers, greet_layer, 0)
    lax.fori_loop(1, widths, greet_width, 0)

    cp_enc.wait()
    cp_ea = [remote(ea_send.at[k], ea_recv.at[k], ea_s.at[k], ea_r.at[k], sib) for k in range(2)]
    for k in range(2):
        cp_x[k].wait()
        ea_send[k] = dot_nn(x[order[k], :], enc[...])
        if k == 0:
            pl.semaphore_wait(barrier, layers - 1 + widths - 1)
        cp_ea[k].start()
    cp_x[2].wait()
    part = dot_nn(x[ynb_rows, :], enc[...])
    cp_ea[0].wait_recv()
    ey_send[...] = part + ea_recv[0]
    cp_ey = remote(ey_send, ey_recv, ey_s.at[0], ey_r.at[0], ynb)
    cp_ey.start()
    cp_x[3].wait()
    part = dot_nn(x[own_rows, :], enc[...])
    cp_ea[1].wait_recv()
    part = part + ea_recv[1]
    cp_ey.wait_recv()
    potential = part + ey_recv[...] + b_ref[...]
    pot[...] = potential
    active = jnp.maximum(potential, 0.0)
    fire[me, own_rows, :] = active.astype(BF16)
    active_sum = jnp.sum(active.reshape(quarter // 8, 8, lat), axis=0)

    pair = lax.div(me, 2)

    @pl.when(lax.rem(me, 2) == 0)
    def _():
        fire[me + 1, own_rows, :] = jnp.zeros((quarter, lat), BF16)

    def fire_copy(src_layer, dst_layer):
        ref = fire.at[src_layer, own_rows, :]
        return remote(ref, ref, fd_s.at[dst_layer], fd_r.at[src_layer], (dst_layer, w))

    def send_fire(m, carry):
        fire_copy(me, m).start()
        return carry

    lax.fori_loop(me + 1, layers, send_fire, 0)

    def fire_pair(p, r, send, recv, where):
        ref = fire.at[pl.ds(2 * p, 2), r, :]
        return remote(ref, ref, send.at[p], recv.at[p], where)

    zero[...] = jnp.zeros(zero.shape, BF16)

    def zero_copy(p):
        return pltpu.make_async_copy(zero, gd_hbm.at[0, pl.ds(2 * p, 2)], out_sems.at[p])

    def send_zero(p, carry):
        zero_copy(p).start()
        return carry

    lax.fori_loop(pair + 1, layers // 2, send_zero, 0)

    def stage_far(p):
        for j in range(2):
            @pl.when(2 * p + j < me)
            def _():
                fire_copy(2 * p + j, me).wait_recv()
        fire_pair(p, own_rows, fy_s, fy_r, ynb).start()
        fire_pair(p, own_rows, fs_s, fs_r, sib).start()

    def stage_y(p):
        fire_pair(p, ynb_rows, fy_s, fy_r, ynb).wait_recv()
        fire_pair(p, ynb_rows, ff_s, ff_r, sib).start()

    cp_t.wait()
    blk = 128 if tokens % 128 == 0 else 16

    def prepare(k, carry):
        r = pl.ds(pl.multiple_of(k * blk, blk), blk)
        acc[r, :] = -t[r, :].astype(F32)
        return carry

    lax.fori_loop(0, tokens // blk, prepare, 0)

    @pl.when(lax.rem(me, 2) == 0)
    def _():
        stage_far(pair)

    for k in range(0, depth, 256):
        xt[k:k + 256, :] = x[:, k:k + 256].T
    cp_dec.wait()

    cols = 512 if depth % 512 == 0 else 128

    def features(p):
        return jnp.concatenate([fire[2 * p], fire[2 * p + 1]], axis=-1)

    def weights(p, at):
        return dec[pl.ds(2 * p, 2), :, at].reshape(2 * lat, -1)

    def forward(i, carry):
        @pl.when((i <= pair) & ((i > 0) | (lax.rem(me, 2) == 1)))
        def _():
            stage_far(pair - i)

        @pl.when((i >= 1) & (i <= pair + 1))
        def _():
            stage_y(pair - i + 1)

        @pl.when(i >= 2)
        def _():
            p = pair - i + 2
            fire_pair(p, sib_rows, fs_s, fs_r, sib).wait_recv()
            fire_pair(p, diag_rows, ff_s, ff_r, sib).wait_recv()
            f = features(p)
            for n in range(0, depth, cols):
                at = slice(n, n + cols)
                acc[:, at] += dot_nn(f, weights(p, at))
            fire_t[p] = f.T
        return carry

    lax.fori_loop(0, pair + 3, forward, 0)

    def finish(k, total):
        r = pl.ds(pl.multiple_of(k * blk, blk), blk)
        m = acc[r, :]
        sig[r, :] = (m * (1.0 / tokens)).astype(BF16)
        sq = jnp.sum((m * m).reshape(blk // 8, 8, depth), axis=0)
        return total + sum(sq[:, n:n + lat] for n in range(0, depth, lat))

    squares = lax.fori_loop(0, tokens // blk, finish, jnp.zeros((8, lat), F32))
    loss_w[w] = 0.5 * squares + SPARSITY * active_sum

    def width_copy(ref, send, recv, src, dst):
        return remote(ref.at[src], ref.at[src], send.at[dst], recv.at[src], (me, dst))

    for k in range(1, widths):
        width_copy(loss_w, lw_s, lw_r, w, lax.rem(w + k, widths)).start()

    own_half = pl.ds(pl.multiple_of(core * half, 16), half)
    sib_half = pl.ds(pl.multiple_of((1 - core) * half, 16), half)
    keep = pl.ds(pl.multiple_of(y * quarter, 16), quarter)
    give = pl.ds(pl.multiple_of((1 - y) * quarter, 16), quarter)

    def c_copy(p):
        return remote(c_send.at[p], c_recv.at[p], cs_s.at[p], cs_r.at[p], sib)

    def cy_copy(p):
        return remote(cy_send.at[p], cy_recv.at[p], cy_s.at[p], cy_r.at[p], ynb)

    def cd_copy(src_layer, dst_layer):
        return remote(
            cd_send.at[dst_layer], cd_recv.at[src_layer], cd_s.at[dst_layer], cd_r.at[src_layer], (dst_layer, w)
        )

    def gd_copy(p):
        return pltpu.make_async_copy(gd.at[pl.ds(2 * p, 2)], gd_hbm.at[0, pl.ds(2 * p, 2)], out_sems.at[p])

    every = slice(0, depth)

    def backward(i, carry):
        @pl.when(i <= pair)
        def _():
            p = i
            out = dot_nt(sig[sib_half, :], weights(p, every)).astype(BF16)
            for j in range(2):
                c_send[p, j] = out[:, j * lat:(j + 1) * lat]
            c_copy(p).start()
            out = dot_nt(sig[own_half, :], weights(p, every))
            for j in range(2):
                c_own[p, j] = out[:, j * lat:(j + 1) * lat]

        @pl.when(i >= 2)
        def _():
            p = i - 2
            c_copy(p).wait_recv()
            for j in range(2):
                cy_send[p, j] = (c_own[p, j, give, :] + c_recv[p, j, give, :].astype(F32)).astype(BF16)
            cy_copy(p).start()
        return carry

    lax.fori_loop(0, pair + 3, backward, 0)

    def outward(i, carry):
        @pl.when(i <= pair)
        def _():
            p = i
            for n in range(0, depth, cols):
                at = slice(n, n + cols)
                gd[pl.ds(2 * p, 2), :, at] = dot_nn(fire_t[p], sig[:, at]).astype(BF16).reshape(2, lat, cols)
            gd_copy(p).start()

        @pl.when(i >= 2)
        def _():
            p = i - 2
            cy_copy(p).wait_recv()
            for j in range(2):
                l = 2 * p + j
                total = c_own[p, j, keep, :] + c_recv[p, j, keep, :].astype(F32) + cy_recv[p, j].astype(F32)

                @pl.when(l < me)
                def _():
                    cd_send[l] = total.astype(BF16)
                    cd_copy(me, l).start()

                @pl.when(l == me)
                def _():
                    fg[...] = total
        return carry

    lax.fori_loop(0, pair + 3, outward, 0)

    for k in range(1, widths):
        width_copy(loss_w, lw_s, lw_r, lax.rem(w + k, widths), w).wait_recv()
    total = loss_w[0]
    for k in range(1, widths):
        total = total + loss_w[k]
    loss_l[me] = total

    def layer_copy(src, dst):
        return remote(loss_l.at[src], loss_l.at[src], ll_s.at[dst], ll_r.at[src], (dst, w))

    def send_loss(k, carry):
        layer_copy(me, lax.rem(me + k, layers)).start()
        return carry

    lax.fori_loop(1, layers, send_loss, 0)

    def gather(m, carry):
        cd_copy(m, me).wait_recv()
        fg[...] += cd_recv[m].astype(F32)
        return carry

    lax.fori_loop(me + 1, layers, gather, 0)

    d = jnp.where(pot[...] > 0, fg[...] + SPARSITY / tokens, 0.0)
    delta[own_rows, :] = d.astype(BF16)

    def delta_copy(r, k, where):
        return remote(delta.at[r, :], delta.at[r, :], dl_s.at[k], dl_r.at[k], where)

    delta_copy(own_rows, 0, ynb).start()
    delta_copy(own_rows, 1, sib).start()
    gb_all[w] = jnp.sum(d.reshape(quarter // 8, 8, lat), axis=0)
    for k in range(1, widths):
        width_copy(gb_all, gb_s, gb_r, w, lax.rem(w + k, widths)).start()
    delta_copy(ynb_rows, 0, ynb).wait_recv()
    delta_copy(ynb_rows, 2, sib).start()

    def take_loss(k, carry):
        layer_copy(lax.rem(me + k, layers), me).wait_recv()
        return carry

    lax.fori_loop(1, layers, take_loss, 0)
    loss = lax.fori_loop(0, layers, lambda k, s: s + loss_l[k], jnp.zeros((8, lat), F32))
    loss_ref[...] = jnp.full((8, lat), jnp.sum(loss) / (tokens * depth * widths * layers), F32)

    delta_copy(sib_rows, 1, sib).wait_recv()
    delta_copy(diag_rows, 2, sib).wait_recv()
    ge_ref[0] = dot_nn(xt[...], delta[...]).astype(BF16)
    for k in range(1, widths):
        width_copy(gb_all, gb_s, gb_r, lax.rem(w + k, widths), w).wait_recv()
    bias = gb_all[0]
    for k in range(1, widths):
        bias = bias + gb_all[k]
    gb_ref[...] = jnp.sum(bias, axis=0, keepdims=True)

    for cp in cp_ea:
        cp.wait_send()
    cp_ey.wait_send()

    def drain_fire(m, carry):
        fire_copy(me, m).wait_send()
        return carry

    lax.fori_loop(me + 1, layers, drain_fire, 0)

    def drain_pair(p, carry):
        fire_pair(p, own_rows, fy_s, fy_r, ynb).wait_send()
        fire_pair(p, own_rows, fs_s, fs_r, sib).wait_send()
        fire_pair(p, ynb_rows, ff_s, ff_r, sib).wait_send()
        c_copy(p).wait_send()
        cy_copy(p).wait_send()
        gd_copy(p).wait()
        return carry

    lax.fori_loop(0, pair + 1, drain_pair, 0)

    def drain_zero(p, carry):
        zero_copy(p).wait()
        return carry

    lax.fori_loop(pair + 1, layers // 2, drain_zero, 0)

    def drain_grad(l, carry):
        cd_copy(me, l).wait_send()
        return carry

    lax.fori_loop(0, me, drain_grad, 0)

    def drain_loss(k, carry):
        layer_copy(me, lax.rem(me + k, layers)).wait_send()
        return carry

    lax.fori_loop(1, layers, drain_loss, 0)
    for k in range(1, widths):
        other = lax.rem(w + k, widths)
        width_copy(loss_w, lw_s, lw_r, w, other).wait_send()
        width_copy(gb_all, gb_s, gb_r, w, other).wait_send()
    delta_copy(own_rows, 0, ynb).wait_send()
    delta_copy(own_rows, 1, sib).wait_send()
    delta_copy(ynb_rows, 2, sib).wait_send()


def copies(cuts, loss_in, ge_in, gb_in, gd_in, loss_out, ge_out, gb_out, gd_out, sems):
    layers = gd_in.shape[1]
    moves = [(ge_in, ge_out), (gb_in, gb_out)]
    for k in range(cuts):
        at = pl.ds(k * (layers // cuts), layers // cuts)
        moves.append((gd_in.at[:, at], gd_out.at[:, at]))
    moves = [pltpu.make_async_copy(a, b, sems.at[k]) for k, (a, b) in enumerate(moves)]
    for m in moves:
        m.start()
    loss_out[0, 0] = loss_in[0, 0]
    for m in moves:
        m.wait()


def hand_out(loss, ge, gb, gd):
    cuts = 4
    anyspace = pl.BlockSpec(memory_space=pl.ANY)
    smem = pl.BlockSpec(memory_space=pltpu.SMEM)
    hbm = pl.BlockSpec(memory_space=pltpu.HBM)
    loss, ge, gb, gd = pl.pallas_call(
        functools.partial(copies, cuts),
        out_shape=(
            jax.ShapeDtypeStruct((1, 1), F32),
            jax.ShapeDtypeStruct(ge.shape, ge.dtype),
            jax.ShapeDtypeStruct(gb.shape, gb.dtype),
            jax.ShapeDtypeStruct(gd.shape, gd.dtype),
        ),
        in_specs=[pl.BlockSpec(memory_space=pltpu.VMEM), anyspace, anyspace, anyspace],
        out_specs=(smem, hbm, hbm, hbm),
        scratch_shapes=[pltpu.SemaphoreType.DMA((cuts + 2,))],
        compiler_params=pltpu.CompilerParams(vmem_limit_bytes=2**20),
        cost_estimate=pl.CostEstimate(
            flops=0, bytes_accessed=4 * (gd.size + ge.size), transcendentals=0
        ),
    )(loss, ge, gb, gd)
    return loss.reshape(()), ge, gb, gd


def per_device(x, t, e, b, d):
    layers, widths = lax.axis_size("layer"), lax.axis_size("width")
    tokens, depth = x.shape[1:]
    lat = e.shape[2]
    half, quarter = tokens // 2, tokens // 4
    pairs = layers // 2
    vmem = pltpu.VMEM
    sem = pltpu.SemaphoreType.DMA
    scratch = [
        vmem((tokens, depth), BF16),
        vmem((depth, tokens), BF16),
        vmem((tokens, depth), BF16),
        vmem((depth, lat), BF16),
        vmem((layers, lat, depth), BF16),
        vmem((tokens, depth), F32),
        vmem((tokens, depth), BF16),
        vmem((layers, tokens, lat), BF16),
        vmem((pairs, 2 * lat, tokens), BF16),
        vmem((quarter, lat), F32),
        vmem((2, quarter, lat), F32),
        vmem((2, quarter, lat), F32),
        vmem((quarter, lat), F32),
        vmem((quarter, lat), F32),
        vmem((pairs, 2, half, lat), BF16),
        vmem((pairs, 2, half, lat), BF16),
        vmem((pairs, 2, half, lat), F32),
        vmem((pairs, 2, quarter, lat), BF16),
        vmem((pairs, 2, quarter, lat), BF16),
        vmem((layers, quarter, lat), BF16),
        vmem((layers, quarter, lat), BF16),
        vmem((quarter, lat), F32),
        vmem((tokens, lat), BF16),
        vmem((widths, 8, lat), F32),
        vmem((widths, 8, lat), F32),
        vmem((layers, 8, lat), F32),
        vmem((layers, lat, depth), BF16),
        vmem((2, lat, depth), BF16),
    ]
    scratch += [
        sem((3,)), sem((4,)), sem((pairs,)), sem((2,)), sem((2,)), sem((1,)), sem((1,)),
        sem((layers,)), sem((layers,)), sem((pairs,)), sem((pairs,)),
        sem((pairs,)), sem((pairs,)), sem((pairs,)), sem((pairs,)),
        sem((pairs,)), sem((pairs,)), sem((pairs,)), sem((pairs,)), sem((layers,)), sem((layers,)),
        sem((3,)), sem((3,)), sem((widths,)), sem((widths,)), sem((widths,)), sem((widths,)),
        sem((layers,)), sem((layers,)),
    ]
    held = sum(math.prod(s.shape) * jnp.dtype(s.dtype).itemsize for s in scratch[:28])
    limit = max(53, min(60, held // 2**20 + 8)) * 2**20
    anyspace = pl.BlockSpec(memory_space=pl.ANY)
    vspace = pl.BlockSpec(memory_space=pltpu.VMEM)
    hbm = pl.BlockSpec(memory_space=pltpu.HBM)
    loss, ge, gb, gd = pl.pallas_call(
        functools.partial(kernel, layers, widths),
        out_shape=(
            jax.ShapeDtypeStruct((8, lat), F32),
            jax.ShapeDtypeStruct((1, depth, lat), BF16),
            jax.ShapeDtypeStruct((1, lat), F32),
            jax.ShapeDtypeStruct((1, layers, lat, depth), BF16),
        ),
        in_specs=[hbm, hbm, hbm, vspace, hbm],
        out_specs=(vspace, vspace, vspace, anyspace),
        scratch_shapes=scratch,
        compiler_params=pltpu.CompilerParams(
            collective_id=0, has_side_effects=True, vmem_limit_bytes=limit
        ),
        cost_estimate=pl.CostEstimate(
            flops=6 * tokens * depth * layers * lat, bytes_accessed=4 * layers * lat * depth, transcendentals=0
        ),
    )(x, t, e, b, d)
    return hand_out(loss, ge, gb, gd)


def solution(mesh):
    return jax.shard_map(
        per_device,
        mesh=mesh,
        in_specs=(
            P("layer", None, "width"),
            P("layer", None, "width"),
            P("layer", "width", None),
            P("layer", None),
            P("layer", None, None, "width"),
        ),
        out_specs=(
            P(),
            P("layer", "width", None),
            P("layer", None),
            P("layer", None, None, "width"),
        ),
        check_vma=False,
    )
```

```python
import functools
import math

import jax
import jax.numpy as jnp
from jax import lax
from jax.experimental import pallas as pl
from jax.experimental.pallas import tpu as pltpu
from jax.sharding import PartitionSpec as P

SPARSITY = 8.0
MESH = pl.DeviceIdType.MESH
F32 = jnp.float32
BF16 = jnp.bfloat16


def dot_nn(a, b):
    return jnp.dot(a, b, preferred_element_type=F32)


def dot_nt(a, b):
    return lax.dot_general(a, b, (((1,), (1,)), ((), ())), preferred_element_type=F32)


def kernel(
    layers, widths,
    x_hbm, t_hbm, e_hbm, b_ref, d_hbm,
    loss_ref, ge_ref, gb_ref, gd_hbm,
    x, xt, t, enc, dec, acc, sig, fire, fire_t, pot,
    ea_send, ea_recv, ey_send, ey_recv,
    c_send, c_recv, c_own, cy_send, cy_recv, cd_send, cd_recv, fg,
    delta, gb_all, loss_w, loss_l, gd, zero,
    in_sems, x_sems, out_sems, ea_s, ea_r, ey_s, ey_r,
    fd_s, fd_r, fy_s, fy_r, fs_s, fs_r, ff_s, ff_r,
    cs_s, cs_r, cy_s, cy_r, cd_s, cd_r,
    dl_s, dl_r, gb_s, gb_r, lw_s, lw_r, ll_s, ll_r,
):
    tokens, depth = x.shape
    lat = enc.shape[1]
    half, quarter = tokens // 2, tokens // 4
    me = lax.axis_index("layer")
    w = lax.axis_index("width")
    core, y = lax.rem(w, 2), lax.div(w, 2)
    sib = (me, w + 1 - 2 * core)
    ynb = (me, w + 2 - 4 * y)

    def rows(c_at, y_at):
        return pl.ds(pl.multiple_of(c_at * half + y_at * quarter, 16), quarter)

    def remote(src, dst, send_sem, recv_sem, where):
        return pltpu.make_async_remote_copy(
            src_ref=src, dst_ref=dst, send_sem=send_sem, recv_sem=recv_sem,
            device_id=where, device_id_type=MESH,
        )

    own_rows = rows(core, y)
    ynb_rows = rows(core, 1 - y)
    sib_rows = rows(1 - core, y)
    diag_rows = rows(1 - core, 1 - y)

    order = (diag_rows, sib_rows, ynb_rows, own_rows)
    cp_enc = pltpu.make_async_copy(e_hbm.at[0], enc, in_sems.at[0])
    cp_enc.start()
    cp_x = [pltpu.make_async_copy(x_hbm.at[0, r], x.at[r], x_sems.at[k]) for k, r in enumerate(order)]
    for cp in cp_x:
        cp.start()
    cp_t = pltpu.make_async_copy(t_hbm.at[0], t, in_sems.at[1])
    cp_t.start()
    cp_dec = pltpu.make_async_copy(d_hbm.at[0], dec, in_sems.at[2])
    cp_dec.start()

    barrier = pltpu.get_barrier_semaphore()

    def greet_layer(k, carry):
        pl.semaphore_signal(barrier, inc=1, device_id=(lax.rem(me + k, layers), w), device_id_type=MESH)
        return carry

    def greet_width(k, carry):
        pl.semaphore_signal(barrier, inc=1, device_id=(me, lax.rem(w + k, widths)), device_id_type=MESH)
        return carry

    lax.fori_loop(1, layers, greet_layer, 0)
    lax.fori_loop(1, widths, greet_width, 0)

    cp_enc.wait()
    cp_ea = [remote(ea_send.at[k], ea_recv.at[k], ea_s.at[k], ea_r.at[k], sib) for k in range(2)]
    for k in range(2):
        cp_x[k].wait()
        ea_send[k] = dot_nn(x[order[k], :], enc[...])
        if k == 0:
            pl.semaphore_wait(barrier, layers - 1 + widths - 1)
        cp_ea[k].start()
    cp_x[2].wait()
    part = dot_nn(x[ynb_rows, :], enc[...])
    cp_ea[0].wait_recv()
    ey_send[...] = part + ea_recv[0]
    cp_ey = remote(ey_send, ey_recv, ey_s.at[0], ey_r.at[0], ynb)
    cp_ey.start()
    cp_x[3].wait()
    part = dot_nn(x[own_rows, :], enc[...])
    cp_ea[1].wait_recv()
    part = part + ea_recv[1]
    cp_ey.wait_recv()
    potential = part + ey_recv[...] + b_ref[...]
    pot[...] = potential
    active = jnp.maximum(potential, 0.0)
    fire[me, own_rows, :] = active.astype(BF16)
    active_sum = jnp.sum(active.reshape(quarter // 8, 8, lat), axis=0)

    pair = lax.div(me, 2)

    @pl.when(lax.rem(me, 2) == 0)
    def _():
        fire[me + 1, own_rows, :] = jnp.zeros((quarter, lat), BF16)

    def fire_copy(src_layer, dst_layer):
        ref = fire.at[src_layer, own_rows, :]
        return remote(ref, ref, fd_s.at[dst_layer], fd_r.at[src_layer], (dst_layer, w))

    def send_fire(m, carry):
        fire_copy(me, m).start()
        return carry

    lax.fori_loop(me + 1, layers, send_fire, 0)

    def fire_pair(p, r, send, recv, where):
        ref = fire.at[pl.ds(2 * p, 2), r, :]
        return remote(ref, ref, send.at[p], recv.at[p], where)

    zero[...] = jnp.zeros(zero.shape, BF16)

    def zero_copy(p):
        return pltpu.make_async_copy(zero, gd_hbm.at[0, pl.ds(2 * p, 2)], out_sems.at[p])

    def send_zero(p, carry):
        zero_copy(p).start()
        return carry

    lax.fori_loop(pair + 1, layers // 2, send_zero, 0)

    def stage_far(p):
        for j in range(2):
            @pl.when(2 * p + j < me)
            def _():
                fire_copy(2 * p + j, me).wait_recv()
        fire_pair(p, own_rows, fy_s, fy_r, ynb).start()
        fire_pair(p, own_rows, fs_s, fs_r, sib).start()

    def stage_y(p):
        fire_pair(p, ynb_rows, fy_s, fy_r, ynb).wait_recv()
        fire_pair(p, ynb_rows, ff_s, ff_r, sib).start()

    @pl.when(lax.rem(me, 2) == 0)
    def _():
        stage_far(pair)

    cp_t.wait()
    blk = 128 if tokens % 128 == 0 else 16

    def prepare(k, carry):
        r = pl.ds(pl.multiple_of(k * blk, blk), blk)
        acc[r, :] = -t[r, :].astype(F32)
        return carry

    lax.fori_loop(0, tokens // blk, prepare, 0)

    cp_dec.wait()

    cols = 512 if depth % 512 == 0 else 128

    def features(p):
        return jnp.concatenate([fire[2 * p], fire[2 * p + 1]], axis=-1)

    def weights(p, at):
        return dec[pl.ds(2 * p, 2), :, at].reshape(2 * lat, -1)

    def forward(i, carry):
        @pl.when((i <= pair) & ((i > 0) | (lax.rem(me, 2) == 1)))
        def _():
            stage_far(pair - i)

        @pl.when((i >= 1) & (i <= pair + 1))
        def _():
            stage_y(pair - i + 1)

        @pl.when(i >= 2)
        def _():
            p = pair - i + 2
            fire_pair(p, sib_rows, fs_s, fs_r, sib).wait_recv()
            fire_pair(p, diag_rows, ff_s, ff_r, sib).wait_recv()
            f = features(p)
            for n in range(0, depth, cols):
                at = slice(n, n + cols)
                acc[:, at] += dot_nn(f, weights(p, at))
            fire_t[p] = f.T
        return carry

    lax.fori_loop(0, pair + 3, forward, 0)

    def finish(k, total):
        r = pl.ds(pl.multiple_of(k * blk, blk), blk)
        m = acc[r, :]
        sig[r, :] = (m * (1.0 / tokens)).astype(BF16)
        sq = jnp.sum((m * m).reshape(blk // 8, 8, depth), axis=0)
        return total + sum(sq[:, n:n + lat] for n in range(0, depth, lat))

    squares = lax.fori_loop(0, tokens // blk, finish, jnp.zeros((8, lat), F32))
    loss_w[w] = 0.5 * squares + SPARSITY * active_sum

    def width_copy(ref, send, recv, src, dst):
        return remote(ref.at[src], ref.at[src], send.at[dst], recv.at[src], (me, dst))

    for k in range(1, widths):
        width_copy(loss_w, lw_s, lw_r, w, lax.rem(w + k, widths)).start()

    own_half = pl.ds(pl.multiple_of(core * half, 16), half)
    sib_half = pl.ds(pl.multiple_of((1 - core) * half, 16), half)
    keep = pl.ds(pl.multiple_of(y * quarter, 16), quarter)
    give = pl.ds(pl.multiple_of((1 - y) * quarter, 16), quarter)

    def c_copy(p):
        return remote(c_send.at[p], c_recv.at[p], cs_s.at[p], cs_r.at[p], sib)

    def cy_copy(p):
        return remote(cy_send.at[p], cy_recv.at[p], cy_s.at[p], cy_r.at[p], ynb)

    def cd_copy(src_layer, dst_layer):
        return remote(
            cd_send.at[dst_layer], cd_recv.at[src_layer], cd_s.at[dst_layer], cd_r.at[src_layer], (dst_layer, w)
        )

    def gd_copy(p):
        return pltpu.make_async_copy(gd.at[pl.ds(2 * p, 2)], gd_hbm.at[0, pl.ds(2 * p, 2)], out_sems.at[p])

    every = slice(0, depth)

    def backward(i, carry):
        @pl.when(i <= pair)
        def _():
            p = i
            out = dot_nt(sig[sib_half, :], weights(p, every)).astype(BF16)
            for j in range(2):
                c_send[p, j] = out[:, j * lat:(j + 1) * lat]
            c_copy(p).start()
            out = dot_nt(sig[own_half, :], weights(p, every))
            for j in range(2):
                c_own[p, j] = out[:, j * lat:(j + 1) * lat]

        @pl.when(i >= 2)
        def _():
            p = i - 2
            c_copy(p).wait_recv()
            for j in range(2):
                cy_send[p, j] = (c_own[p, j, give, :] + c_recv[p, j, give, :].astype(F32)).astype(BF16)
            cy_copy(p).start()
        return carry

    lax.fori_loop(0, pair + 3, backward, 0)

    def outward(i, carry):
        @pl.when(i <= pair)
        def _():
            p = i
            for n in range(0, depth, cols):
                at = slice(n, n + cols)
                gd[pl.ds(2 * p, 2), :, at] = dot_nn(fire_t[p], sig[:, at]).astype(BF16).reshape(2, lat, cols)
            gd_copy(p).start()

        @pl.when(i >= 2)
        def _():
            p = i - 2
            cy_copy(p).wait_recv()
            for j in range(2):
                l = 2 * p + j
                total = c_own[p, j, keep, :] + c_recv[p, j, keep, :].astype(F32) + cy_recv[p, j].astype(F32)

                @pl.when(l < me)
                def _():
                    cd_send[l] = total.astype(BF16)
                    cd_copy(me, l).start()

                @pl.when(l == me)
                def _():
                    fg[...] = total
        return carry

    lax.fori_loop(0, pair + 3, outward, 0)

    for k in range(1, widths):
        width_copy(loss_w, lw_s, lw_r, lax.rem(w + k, widths), w).wait_recv()
    total = loss_w[0]
    for k in range(1, widths):
        total = total + loss_w[k]
    loss_l[me] = total

    def layer_copy(src, dst):
        return remote(loss_l.at[src], loss_l.at[src], ll_s.at[dst], ll_r.at[src], (dst, w))

    def send_loss(k, carry):
        layer_copy(me, lax.rem(me + k, layers)).start()
        return carry

    lax.fori_loop(1, layers, send_loss, 0)

    for k in range(0, depth, 256):
        xt[k:k + 256, :] = x[:, k:k + 256].T

    def gather(m, carry):
        cd_copy(m, me).wait_recv()
        fg[...] += cd_recv[m].astype(F32)
        return carry

    lax.fori_loop(me + 1, layers, gather, 0)

    d = jnp.where(pot[...] > 0, fg[...] + SPARSITY / tokens, 0.0)
    delta[own_rows, :] = d.astype(BF16)

    def delta_copy(r, k, where):
        return remote(delta.at[r, :], delta.at[r, :], dl_s.at[k], dl_r.at[k], where)

    delta_copy(own_rows, 0, ynb).start()
    delta_copy(own_rows, 1, sib).start()
    gb_all[w] = jnp.sum(d.reshape(quarter // 8, 8, lat), axis=0)
    for k in range(1, widths):
        width_copy(gb_all, gb_s, gb_r, w, lax.rem(w + k, widths)).start()
    delta_copy(ynb_rows, 0, ynb).wait_recv()
    delta_copy(ynb_rows, 2, sib).start()

    def take_loss(k, carry):
        layer_copy(lax.rem(me + k, layers), me).wait_recv()
        return carry

    lax.fori_loop(1, layers, take_loss, 0)
    loss = lax.fori_loop(0, layers, lambda k, s: s + loss_l[k], jnp.zeros((8, lat), F32))
    loss_ref[...] = jnp.full((8, lat), jnp.sum(loss) / (tokens * depth * widths * layers), F32)

    delta_copy(sib_rows, 1, sib).wait_recv()
    delta_copy(diag_rows, 2, sib).wait_recv()
    ge_ref[0] = dot_nn(xt[...], delta[...]).astype(BF16)
    for k in range(1, widths):
        width_copy(gb_all, gb_s, gb_r, lax.rem(w + k, widths), w).wait_recv()
    bias = gb_all[0]
    for k in range(1, widths):
        bias = bias + gb_all[k]
    gb_ref[...] = jnp.sum(bias, axis=0, keepdims=True)

    for cp in cp_ea:
        cp.wait_send()
    cp_ey.wait_send()

    def drain_fire(m, carry):
        fire_copy(me, m).wait_send()
        return carry

    lax.fori_loop(me + 1, layers, drain_fire, 0)

    def drain_pair(p, carry):
        fire_pair(p, own_rows, fy_s, fy_r, ynb).wait_send()
        fire_pair(p, own_rows, fs_s, fs_r, sib).wait_send()
        fire_pair(p, ynb_rows, ff_s, ff_r, sib).wait_send()
        c_copy(p).wait_send()
        cy_copy(p).wait_send()
        gd_copy(p).wait()
        return carry

    lax.fori_loop(0, pair + 1, drain_pair, 0)

    def drain_zero(p, carry):
        zero_copy(p).wait()
        return carry

    lax.fori_loop(pair + 1, layers // 2, drain_zero, 0)

    def drain_grad(l, carry):
        cd_copy(me, l).wait_send()
        return carry

    lax.fori_loop(0, me, drain_grad, 0)

    def drain_loss(k, carry):
        layer_copy(me, lax.rem(me + k, layers)).wait_send()
        return carry

    lax.fori_loop(1, layers, drain_loss, 0)
    for k in range(1, widths):
        other = lax.rem(w + k, widths)
        width_copy(loss_w, lw_s, lw_r, w, other).wait_send()
        width_copy(gb_all, gb_s, gb_r, w, other).wait_send()
    delta_copy(own_rows, 0, ynb).wait_send()
    delta_copy(own_rows, 1, sib).wait_send()
    delta_copy(ynb_rows, 2, sib).wait_send()


def copies(cuts, loss_in, ge_in, gb_in, gd_in, loss_out, ge_out, gb_out, gd_out, sems):
    layers = gd_in.shape[1]
    moves = [(ge_in, ge_out), (gb_in, gb_out)]
    for k in range(cuts):
        at = pl.ds(k * (layers // cuts), layers // cuts)
        moves.append((gd_in.at[:, at], gd_out.at[:, at]))
    moves = [pltpu.make_async_copy(a, b, sems.at[k]) for k, (a, b) in enumerate(moves)]
    for m in moves:
        m.start()
    loss_out[0, 0] = loss_in[0, 0]
    for m in moves:
        m.wait()


def hand_out(loss, ge, gb, gd):
    cuts = 4
    anyspace = pl.BlockSpec(memory_space=pl.ANY)
    smem = pl.BlockSpec(memory_space=pltpu.SMEM)
    hbm = pl.BlockSpec(memory_space=pltpu.HBM)
    loss, ge, gb, gd = pl.pallas_call(
        functools.partial(copies, cuts),
        out_shape=(
            jax.ShapeDtypeStruct((1, 1), F32),
            jax.ShapeDtypeStruct(ge.shape, ge.dtype),
            jax.ShapeDtypeStruct(gb.shape, gb.dtype),
            jax.ShapeDtypeStruct(gd.shape, gd.dtype),
        ),
        in_specs=[pl.BlockSpec(memory_space=pltpu.VMEM), anyspace, anyspace, anyspace],
        out_specs=(smem, hbm, hbm, hbm),
        scratch_shapes=[pltpu.SemaphoreType.DMA((cuts + 2,))],
        compiler_params=pltpu.CompilerParams(vmem_limit_bytes=2**20),
        cost_estimate=pl.CostEstimate(
            flops=0, bytes_accessed=4 * (gd.size + ge.size), transcendentals=0
        ),
    )(loss, ge, gb, gd)
    return loss.reshape(()), ge, gb, gd


def per_device(x, t, e, b, d):
    layers, widths = lax.axis_size("layer"), lax.axis_size("width")
    tokens, depth = x.shape[1:]
    lat = e.shape[2]
    half, quarter = tokens // 2, tokens // 4
    pairs = layers // 2
    vmem = pltpu.VMEM
    sem = pltpu.SemaphoreType.DMA
    scratch = [
        vmem((tokens, depth), BF16),
        vmem((depth, tokens), BF16),
        vmem((tokens, depth), BF16),
        vmem((depth, lat), BF16),
        vmem((layers, lat, depth), BF16),
        vmem((tokens, depth), F32),
        vmem((tokens, depth), BF16),
        vmem((layers, tokens, lat), BF16),
        vmem((pairs, 2 * lat, tokens), BF16),
        vmem((quarter, lat), F32),
        vmem((2, quarter, lat), F32),
        vmem((2, quarter, lat), F32),
        vmem((quarter, lat), F32),
        vmem((quarter, lat), F32),
        vmem((pairs, 2, half, lat), BF16),
        vmem((pairs, 2, half, lat), BF16),
        vmem((pairs, 2, half, lat), F32),
        vmem((pairs, 2, quarter, lat), BF16),
        vmem((pairs, 2, quarter, lat), BF16),
        vmem((layers, quarter, lat), BF16),
        vmem((layers, quarter, lat), BF16),
        vmem((quarter, lat), F32),
        vmem((tokens, lat), BF16),
        vmem((widths, 8, lat), F32),
        vmem((widths, 8, lat), F32),
        vmem((layers, 8, lat), F32),
        vmem((layers, lat, depth), BF16),
        vmem((2, lat, depth), BF16),
    ]
    scratch += [
        sem((3,)), sem((4,)), sem((pairs,)), sem((2,)), sem((2,)), sem((1,)), sem((1,)),
        sem((layers,)), sem((layers,)), sem((pairs,)), sem((pairs,)),
        sem((pairs,)), sem((pairs,)), sem((pairs,)), sem((pairs,)),
        sem((pairs,)), sem((pairs,)), sem((pairs,)), sem((pairs,)), sem((layers,)), sem((layers,)),
        sem((3,)), sem((3,)), sem((widths,)), sem((widths,)), sem((widths,)), sem((widths,)),
        sem((layers,)), sem((layers,)),
    ]
    held = sum(math.prod(s.shape) * jnp.dtype(s.dtype).itemsize for s in scratch[:28])
    limit = max(53, min(60, held // 2**20 + 8)) * 2**20
    anyspace = pl.BlockSpec(memory_space=pl.ANY)
    vspace = pl.BlockSpec(memory_space=pltpu.VMEM)
    hbm = pl.BlockSpec(memory_space=pltpu.HBM)
    loss, ge, gb, gd = pl.pallas_call(
        functools.partial(kernel, layers, widths),
        out_shape=(
            jax.ShapeDtypeStruct((8, lat), F32),
            jax.ShapeDtypeStruct((1, depth, lat), BF16),
            jax.ShapeDtypeStruct((1, lat), F32),
            jax.ShapeDtypeStruct((1, layers, lat, depth), BF16),
        ),
        in_specs=[hbm, hbm, hbm, vspace, hbm],
        out_specs=(vspace, vspace, vspace, anyspace),
        scratch_shapes=scratch,
        compiler_params=pltpu.CompilerParams(
            collective_id=0, has_side_effects=True, vmem_limit_bytes=limit
        ),
        cost_estimate=pl.CostEstimate(
            flops=6 * tokens * depth * layers * lat, bytes_accessed=4 * layers * lat * depth, transcendentals=0
        ),
    )(x, t, e, b, d)
    return hand_out(loss, ge, gb, gd)


def solution(mesh):
    return jax.shard_map(
        per_device,
        mesh=mesh,
        in_specs=(
            P("layer", None, "width"),
            P("layer", None, "width"),
            P("layer", "width", None),
            P("layer", None),
            P("layer", None, None, "width"),
        ),
        out_specs=(
            P(),
            P("layer", "width", None),
            P("layer", None),
            P("layer", None, None, "width"),
        ),
        check_vma=False,
    )
```
